32 devices in a mesh: expert: 16 (over z, x, core), fsdp: 2 (over y).
Axes of the slice: x: 2, y: 2, z: 4, core: 2. Of those that a mesh axis runs over, the one named last changes fastest.
Arguments:
- teacher_in: bfloat16 [2048, 4096], P('expert'), may hold values from -6 to 6
- routes: int32 [2048, 8], P('expert'), may hold values from 0 to 15, all different within a row; in each aligned block of 128 rows (0 to 127, 128 to 255, ...) at most 72 rows name the same one
- route_weights: float32 [2048, 8], P('expert'), may hold values from 0.1 to 0.5
- expert_gate_up: bfloat16 [16, 4096, 2, 1024], P('expert', None, None, 'fsdp'), may hold values from -0.09375 to 0.09375
- expert_down: bfloat16 [16, 1024, 4096], P('expert', 'fsdp'), may hold values from -0.1875 to 0.1875
- student_in: bfloat16 [2048, 2048], P('expert'), may hold values from -6 to 6
- norm_gain: float32 [2048], replicated, may hold values from 0.5 to 2
- projector: bfloat16 [2048, 4096], P(None, 'fsdp'), may hold values from -0.125 to 0.125
- second_moment: float32 [2048, 4096], P('expert', 'fsdp'), may hold values from 512 to 8192
Outputs:
- d_student: bfloat16 [2048, 2048], P('expert')
- proj_step: float32 [2048, 4096], P('expert', 'fsdp')
The draws below stay inside these ranges and needn't reach their ends.
Inputs may be any that keep to these rules, and one draw needn't show every extreme that they name: `routes`: each row names 8 different experts; in each block of 128 consecutive rows (the rows of one index of expert) no expert is named by more than 72 rows.
All inputs are finite; a program needn't handle non-finite values.
Results may differ from the reference program's by a relative error of at most 0.02.
Values may be sent and summed in bfloat16 or wider, within the bound.
No kernel may reach another device: no remote copies, remote signals or barrier semaphores. Data moves between devices by JAX's collectives and lax.ppermute only.
A program may use at most 128 MiB of HBM per device.

```python
import math
import jax
import jax.numpy as jnp
import numpy as np
from jax import lax

DT = 4096
TH = 1024
DS = 2048
TOPK = 8
TG = 128
EXPERTS = 16
CAP = 72
TOKENS = 2048
N_EXPERT = 16
N_FSDP = 2


def strengthened(array, rng, source, target, shards_of, factor):
    owner, partner = [(jnp.arange(array.shape[dim]) // (array.shape[dim] // shards_of)).reshape([-1 if axis == dim else 1 for axis in range(array.ndim)]) for dim in (source, target)]
    chosen = jax.random.permutation(rng, shards_of)[partner]
    strong = (owner == chosen) | (owner == (partner + shards_of // 2) % shards_of)
    return jnp.where(strong, factor * array, array)


def shard_levels(stream_key, shape, shards, low, top_value):
    def one(dim, blocks):
        heights = jax.random.uniform(jax.random.fold_in(jax.random.fold_in(stream_key, 6), dim), (blocks,), jnp.float32, low / len(shards), top_value / len(shards))
        return jnp.repeat(jnp.exp(heights), shape[dim] // blocks).reshape((-1,) + (1,) * (len(shape) - dim - 1))

    loudness = one(*shards[0])
    for cut in shards[1:]:
        loudness = loudness * one(*cut)
    return loudness


def assign_block(rng, own, number, rows, count, top, bound, skew):
    order = jax.random.permutation(rng, count)
    crowded, usual = shares(count, rows * top, bound, skew, True), shares(count, rows * top, bound, skew, False)
    places = jnp.arange(count)

    def named(sizes, turn):
        used = int((sizes > 0).sum())
        fixed = max(1, used // 4)
        passed = fixed + (places - fixed + turn * (used - fixed)) % max(1, count - fixed)
        return jnp.zeros((count,), jnp.int32).at[order[jnp.where(places < fixed, places, passed)]].set(jnp.asarray(sizes, jnp.int32))

    sizes = jnp.where(number % 4 == 0, named(crowded, number // 4), named(usual, number - number // 4 - 1))
    mixed = jax.random.permutation(jax.random.fold_in(own, 3), count)
    donor, receiver = mixed[0:count // 2 * 2:2], mixed[1:count // 2 * 2:2]
    margin = jnp.minimum(sizes[donor] - 1, bound - sizes[receiver]) // 2
    margin = jnp.where((donor == order[0]) | (receiver == order[0]) | (sizes[receiver] == 0), 0, jnp.maximum(margin, 0))
    passed = jax.random.randint(jax.random.fold_in(own, 4), (count // 2,), 0, 1 << 20) % (margin + 1)
    sizes = sizes.at[donor].add(-passed).at[receiver].add(passed)
    labels = jnp.searchsorted(jnp.cumsum(sizes), jnp.arange(rows * top), side="right").astype(jnp.int32)
    listing = labels.reshape(top, rows).T
    listing = listing[jax.random.permutation(jax.random.fold_in(own, 1), rows)]
    turn = jax.random.randint(jax.random.fold_in(own, 2), (rows, 1), 0, top)
    return jnp.take_along_axis(listing, (jnp.arange(top)[None, :] + turn) % top, axis=1)


def shares(count, total, most, skew, full):
    weights = [(1 << 20) // math.isqrt(standing ** skew) + 1 for standing in range(1, count + 1)]
    largest = most if full else min(most, max(-(-total // count), total * weights[0] // sum(weights)))
    least = 1 if total - largest >= count - 1 else 0
    holding, rest = [largest] + [least] * (count - 1), total - largest - least * (count - 1)
    while rest > 0:
        free = [i for i in range(1, count) if holding[i] < largest] or [i for i in range(1, count) if holding[i] < most]
        pool, budget = sum([weights[i] for i in free]), rest
        for i in free:
            more = min(most - holding[i], max(1, budget * weights[i] // pool), rest)
            holding[i] = holding[i] + more
            rest = rest - more
    return np.array(holding)


def noise(stream_key, shape, deviation, limit, pieces=(), kind=jnp.bfloat16):
    loudness = shard_levels(stream_key, shape, pieces, -0.22, 0.18) if pieces else 1.0
    result = jax.random.normal(stream_key, shape, jnp.float32) * deviation * loudness
    return jnp.minimum(jnp.maximum(result, -limit), limit).astype(kind)


def noise_with(own_key, extent, scale, bound, cuts, heavy, kind=jnp.bfloat16):
    drawn = scale * jax.random.normal(own_key, extent, jnp.float32)
    if cuts:
        drawn = drawn * shard_levels(own_key, extent, cuts, -0.22, 0.18)
    return jnp.clip(strengthened(drawn, jax.random.fold_in(own_key, 3), *heavy), -bound, bound).astype(kind)


def setup_inputs(seed: int = 0) -> dict:
    streams_of = jax.random.split(jax.random.key(seed), 10)
    teacher_in = noise(streams_of[0], (TOKENS, DT), 1.0, 6.0, ((0, 16),))
    routes_keys = jax.random.split(jax.random.fold_in(streams_of[1], 1), TOKENS // TG)
    routes_turns = jax.random.permutation(jax.random.fold_in(streams_of[1], 3), TOKENS // TG)
    routes = jax.vmap(lambda own, number: assign_block(jax.random.fold_in(streams_of[1], 2), own, number, TG, EXPERTS, TOPK, CAP, 1))(routes_keys, routes_turns).reshape((TOKENS, TOPK))
    route_weights = jnp.clip(0.1 + 0.4 * jax.random.uniform(streams_of[2], (TOKENS, TOPK), jnp.float32) ** shard_levels(streams_of[2], (TOKENS, TOPK), ((0, 16),), -0.2, 0.2), 0.1, 0.5)
    expert_gate_up = noise(streams_of[3], (EXPERTS, DT, 2, TH), DT ** -0.5, 0.09375, ((0, 16), (3, 2)))
    expert_down = noise(streams_of[4], (EXPERTS, TH, DT), TH ** -0.5, 0.1875, ((0, 16), (1, 2)))
    student_in = noise_with(streams_of[5], (TOKENS, DS), 1.0, 6.0, ((0, 16),), (0, 1, 16, 2.0))
    norm_gain = jnp.clip(jnp.exp(jax.random.uniform(streams_of[6], (DS,), jnp.float32, math.log(0.5), math.log(2.0))), 0.5, 2.0)
    projector = noise(streams_of[7], (DS, DT), DS ** -0.5, 0.125, ((1, 2),))
    second_moment = jnp.clip(jnp.exp(math.log(8192.0) - 2.7725887 * jax.random.uniform(streams_of[8], (DS, DT), jnp.float32) ** shard_levels(streams_of[8], (DS, DT), ((0, 16), (1, 2)), -0.2, 0.2)), 512.0, 8192.0)
    return {"teacher_in": teacher_in, "routes": routes, "route_weights": route_weights, "expert_gate_up": expert_gate_up, "expert_down": expert_down, "student_in": student_in, "norm_gain": norm_gain, "projector": projector, "second_moment": second_moment}


beta_two = 0.95

def block_targets(block_routes):
    flatten = block_routes.reshape(-1)
    onehot = (flatten[:, None] == jnp.arange(EXPERTS, dtype=jnp.int32)[None, :]).astype(jnp.int32)
    before = jnp.cumsum(onehot, axis=0) - onehot
    position = lax.optimization_barrier(jnp.sum(before * onehot, axis=1))
    return (flatten * CAP + position).astype(jnp.int32)

def expert_block(token_rows, gate_up, down_rows):
    gate_up_out = jnp.dot(token_rows, gate_up.reshape(DT, 2 * TH), preferred_element_type=jnp.float32)
    hidden = (jax.nn.silu(gate_up_out[:, :TH]) * gate_up_out[:, TH:]).astype(jnp.bfloat16)
    block_width = TH // N_FSDP
    summed = jnp.zeros((token_rows.shape[0], DT), jnp.float32)
    for quarter in range(N_FSDP):
        partial_out = jnp.dot(hidden[:, quarter * block_width:(quarter + 1) * block_width], down_rows[quarter * block_width:(quarter + 1) * block_width], preferred_element_type=jnp.float32)
        rounded = lax.optimization_barrier(partial_out.astype(jnp.bfloat16))
        summed = summed + rounded.astype(jnp.float32)
    return summed

def invert_block(target_row, token_row, weight_row):
    slot_token = jnp.full((EXPERTS * CAP,), TOKENS, jnp.int32).at[target_row].set(token_row)
    slot_weight = jnp.zeros((EXPERTS * CAP,), jnp.float32).at[target_row].set(weight_row)
    return (slot_token, slot_weight)

def reference(teacher_in, routes, route_weights, expert_gate_up, expert_down, student_in, norm_gain, projector, second_moment):
    blocks = routes.reshape(N_EXPERT, TG * TOPK)
    targets = jax.vmap(block_targets)(blocks)
    local_token = (jnp.arange(TG * TOPK, dtype=jnp.int32) // TOPK).astype(jnp.int32)
    block_start = (jnp.arange(N_EXPERT, dtype=jnp.int32) * TG).astype(jnp.int32)
    global_token = (local_token[None, :] + block_start[:, None]).astype(jnp.int32)
    weights_flat = route_weights.reshape(N_EXPERT, TG * TOPK)
    slot_token, slot_weight = jax.vmap(invert_block)(targets, global_token, weights_flat)
    slot_token = slot_token.reshape(N_EXPERT, EXPERTS, CAP).transpose(1, 0, 2).reshape(EXPERTS, N_EXPERT * CAP)
    slot_weight = slot_weight.reshape(N_EXPERT, EXPERTS, CAP).transpose(1, 0, 2).reshape(EXPERTS, N_EXPERT * CAP)
    padded = jnp.concatenate([teacher_in, jnp.zeros((1, DT), teacher_in.dtype)], axis=0)

    def one_expert(carry, inputs):
        gate_up, down_rows, tokens_here, weights_here = inputs
        expert_out = expert_block(padded[tokens_here], gate_up, down_rows)
        return (carry.at[tokens_here].add(weights_here[:, None] * expert_out), None)
    teacher, _ = lax.scan(one_expert, jnp.zeros((TOKENS + 1, DT), jnp.float32), (expert_gate_up, expert_down, slot_token, slot_weight))
    teacher = teacher[:TOKENS]
    student_wide = student_in.astype(jnp.float32)
    inv_rms = lax.rsqrt(lax.optimization_barrier(jnp.mean(student_wide * student_wide, axis=1, keepdims=True)) + 1e-06)
    normed = student_wide * inv_rms
    student_feat = (normed * norm_gain[None, :]).astype(jnp.bfloat16)
    residue = (jnp.dot(student_feat, projector, preferred_element_type=jnp.float32) - teacher).astype(jnp.bfloat16)
    feat_grad = jnp.dot(residue, projector.T, preferred_element_type=jnp.float32)
    scaled = feat_grad * norm_gain[None, :]
    d_student = (inv_rms * (scaled - normed * lax.optimization_barrier(jnp.mean(scaled * normed, axis=1, keepdims=True)))).astype(jnp.bfloat16)
    proj_grad = jnp.dot(student_feat.T, residue, preferred_element_type=jnp.float32)
    proj_step = proj_grad / jnp.sqrt(beta_two * second_moment + (1.0 - beta_two) * proj_grad * proj_grad)
    return (d_student, proj_step)
```

```python
import jax
import jax.numpy as jnp
from jax import lax
from jax.sharding import PartitionSpec as P

beta_two = 0.95
CORES = 2


def ring_order(chips):
    return list(range(0, chips, 2)) + list(range(1, chips, 2))[::-1]


def moves(chips):
    ring = ring_order(chips)

    def shift(by):
        return [
            (CORES * ring[i] + core, CORES * ring[(i + by) % chips] + core)
            for i in range(chips)
            for core in range(CORES)
        ]

    swap = [(i, i ^ 1) for i in range(CORES * chips)]
    return ring, shift, swap


def dense_weights(routes, route_weights, experts):
    hit = routes[:, :, None] == jnp.arange(experts, dtype=jnp.int32)[None, None, :]
    return jnp.sum(jnp.where(hit, route_weights[:, :, None], 0.0), axis=1)


def per_device(
    teacher_in,
    routes,
    route_weights,
    expert_gate_up,
    expert_down,
    student_in,
    norm_gain,
    projector,
    second_moment,
):
    bf16, f32 = jnp.bfloat16, jnp.float32
    experts, shares = lax.axis_size("expert"), lax.axis_size("fsdp")
    chips = experts // CORES
    ring, shift, swap = moves(chips)
    right, left = shift(1), shift(-1)
    tokens_here, half = teacher_in.shape[0], teacher_in.shape[0] // 2
    columns = projector.shape[1]
    features = student_in.shape[1]
    hidden_units = expert_down.shape[1]

    me = lax.axis_index("expert")
    core = me % CORES
    share = lax.axis_index("fsdp")
    ring_table = jnp.asarray(ring, jnp.int32)
    place_table = jnp.asarray([ring.index(q) for q in range(chips)], jnp.int32)
    place = place_table[me // CORES]

    def fsdp_shift(value, by):
        return lax.ppermute(value, "fsdp", [(i, (i + by) % shares) for i in range(shares)])

    mine = dense_weights(routes, route_weights, experts).T
    table = lax.all_gather(mine, "expert", axis=0, tiled=False)
    table = lax.dynamic_index_in_dim(table, me, axis=1, keepdims=False)
    table = table.reshape(experts * 2, half)
    steps = jnp.arange(chips, dtype=jnp.int32)
    behind = ring_table[(place - steps) % chips]
    ahead = ring_table[(place + steps) % chips]
    rows = jnp.stack(
        [
            (CORES * behind + core) * 2,
            (CORES * ahead + core) * 2 + 1,
            (CORES * behind + 1 - core) * 2,
            (CORES * ahead + 1 - core) * 2 + 1,
        ],
        axis=1,
    )
    weights = table[rows].reshape(chips, CORES * tokens_here)

    gate_up = expert_gate_up.reshape(expert_gate_up.shape[1], -1)
    down = expert_down[0]

    def down_columns(owner):
        return lax.dynamic_slice_in_dim(down, owner * columns, columns, axis=1)

    down_rows = [down_columns(share)]
    for by in range(1, shares):
        down_rows.append(fsdp_shift(down_columns((share + by) % shares), by))
    down_rows = jnp.concatenate(down_rows, axis=0)

    student_wide = student_in.astype(f32)
    inv_rms = lax.rsqrt(jnp.mean(student_wide * student_wide, axis=1, keepdims=True) + 1e-06)
    normed = student_wide * inv_rms
    student_feat = (normed * norm_gain[None, :]).astype(bf16)
    projected = jnp.dot(student_feat, projector, preferred_element_type=f32)

    chip_features = features // chips

    def feature_columns(chip):
        return lax.dynamic_slice_in_dim(student_feat, chip * chip_features, chip_features, axis=1)

    feat_from = [feature_columns(ring_table[place])]
    for by in range(1, chips):
        piece = feature_columns(ring_table[(place + by) % chips])
        feat_from.append(lax.ppermute(piece, "expert", shift(by)))

    def contribution(rows_here, weight):
        both = jnp.concatenate([rows_here, lax.ppermute(rows_here, "expert", swap)], axis=0)
        gate_up_out = jnp.dot(both, gate_up, preferred_element_type=f32)
        gate, up = gate_up_out[:, :hidden_units], gate_up_out[:, hidden_units:]
        hidden = (jax.nn.silu(gate) * up * weight[:, None]).astype(bf16)
        whole = [hidden] + [fsdp_shift(hidden, by) for by in range(1, shares)]
        out = jnp.dot(jnp.concatenate(whole, axis=1), down_rows, preferred_element_type=f32)
        other = lax.ppermute(out[tokens_here:].astype(bf16), "expert", swap)
        return out[:tokens_here] + other.astype(f32)

    own = contribution(teacher_in, weights[0])
    ahead_rows, behind_rows = teacher_in[:half], teacher_in[half:]
    ahead_sum = behind_sum = None
    for step in range(1, chips):
        ahead_rows = lax.ppermute(ahead_rows, "expert", right)
        behind_rows = lax.ppermute(behind_rows, "expert", left)
        part = contribution(jnp.concatenate([ahead_rows, behind_rows], axis=0), weights[step])
        ahead_part, behind_part = part[:half], part[half:]
        if step > 1:
            ahead_part = ahead_part + ahead_sum.astype(f32)
            behind_part = behind_part + behind_sum.astype(f32)
        ahead_sum = lax.ppermute(ahead_part.astype(bf16), "expert", right)
        behind_sum = lax.ppermute(behind_part.astype(bf16), "expert", left)
    teacher = own + jnp.concatenate([ahead_sum, behind_sum], axis=0).astype(f32)
    residue = (projected - teacher).astype(bf16)

    feat_part = jnp.einsum("tc,dc->td", residue, projector, preferred_element_type=f32).astype(bf16)
    feat_grad = feat_part.astype(f32)
    for by in range(1, shares):
        feat_grad = feat_grad + fsdp_shift(feat_part, by).astype(f32)
    scaled = feat_grad * norm_gain[None, :]
    d_student = (
        inv_rms * (scaled - normed * jnp.mean(scaled * normed, axis=1, keepdims=True))
    ).astype(bf16)

    ahead_rows, behind_rows = residue[:half], residue[half:]
    residues, feats = [residue], [feat_from[0]]
    for step in range(1, chips):
        ahead_rows = lax.ppermute(ahead_rows, "expert", right)
        behind_rows = lax.ppermute(behind_rows, "expert", left)
        residues += [ahead_rows, behind_rows]
        feats += [feat_from[step][:half], feat_from[chips - step][half:]]
    grad = jnp.einsum(
        "tr,tc->rc",
        jnp.concatenate(feats, axis=0),
        jnp.concatenate(residues, axis=0),
        preferred_element_type=f32,
    )
    block = chip_features // CORES
    kept = lax.dynamic_slice_in_dim(grad, core * block, block, axis=0)
    given = lax.dynamic_slice_in_dim(grad, (1 - core) * block, block, axis=0)
    grad_block = kept + lax.ppermute(given, "expert", swap)
    proj_step = grad_block / jnp.sqrt(
        beta_two * second_moment + (1.0 - beta_two) * grad_block * grad_block
    )
    return (d_student, proj_step)


def solution(mesh):
    placed = (
        P("expert", None),
        P("expert", None),
        P("expert", None),
        P("expert", None, None, "fsdp"),
        P("expert", "fsdp", None),
        P("expert", None),
        P(),
        P(None, "fsdp"),
        P("expert", "fsdp"),
    )
    return jax.shard_map(
        per_device,
        mesh=mesh,
        in_specs=placed,
        out_specs=(P("expert", None), P("expert", "fsdp")),
        check_vma=False,
    )
```

```python
import jax
import jax.numpy as jnp
from jax import lax
from jax.experimental import pallas as pl
from jax.experimental.pallas import tpu as pltpu
from jax.sharding import PartitionSpec as P

beta_two = 0.95
CORES = 2


def ring_order(chips):
    return list(range(0, chips, 2)) + list(range(1, chips, 2))[::-1]


def moves(chips):
    ring = ring_order(chips)
    around = []
    for i in range(chips):
        around.append((CORES * ring[i], CORES * ring[(i + 1) % chips]))
        around.append((CORES * ring[i] + 1, CORES * ring[i - 1] + 1))
    back = [(to, source) for source, to in around]
    return ring, around, back, [(i, i ^ 1) for i in range(CORES * chips)]


def fence(values):
    return lax.optimization_barrier(values)


def rows_with_weights(tokens, routes, route_weights, experts, lanes):
    lane = lax.broadcasted_iota(jnp.int32, (routes.shape[0], lanes), 1)
    weight = jnp.zeros((routes.shape[0], lanes), jnp.float32)
    for k in range(routes.shape[1]):
        hit = (lane == routes[:, k : k + 1]) | (lane == routes[:, k : k + 1] + experts)
        weight = weight + jnp.where(hit, route_weights[:, k : k + 1], 0.0)
    high = weight.astype(jnp.bfloat16)
    low = (weight - high.astype(jnp.float32)).astype(jnp.bfloat16)
    return jnp.concatenate([tokens, jnp.where(lane < experts, high, low)], axis=1)


def hidden_kernel(who, gates, ups, *refs, experts):
    rows, hidden = refs[:-1], refs[-1]
    tokens, width = rows[0].shape[0], gates.shape[0]
    lane = lax.broadcasted_iota(jnp.int32, (tokens, rows[0].shape[1] - width), 1)
    mine = (lane == who[0]) | (lane == who[0] + experts)
    for index, block in enumerate(rows):
        gate = jnp.dot(block[:, :width], gates[...], preferred_element_type=jnp.float32)
        up = jnp.dot(block[:, :width], ups[...], preferred_element_type=jnp.float32)
        weight = jnp.where(mine, block[:, width:].astype(jnp.float32), 0.0)
        weight = jnp.sum(weight, axis=1, keepdims=True)
        out = gate / (1.0 + jnp.exp(-gate)) * up * weight
        hidden[index * tokens : (index + 1) * tokens] = out.astype(hidden.dtype)


def hidden_of(who, weights, rows, experts):
    width, both = weights.shape
    tokens, count = rows[0].shape[0], len(rows)
    tile = min(both // 2, 256)
    tiles = both // 2 // tile
    return pl.pallas_call(
        lambda *refs: hidden_kernel(*refs, experts=experts),
        out_shape=jax.ShapeDtypeStruct((count * tokens, both // 2), jnp.bfloat16),
        grid_spec=pltpu.PrefetchScalarGridSpec(
            num_scalar_prefetch=1,
            grid=(tiles,),
            in_specs=[
                pl.BlockSpec((width, tile), lambda j, who: (0, j)),
                pl.BlockSpec((width, tile), lambda j, who: (0, tiles + j)),
                *[pl.BlockSpec(block.shape, lambda j, who: (0, 0)) for block in rows],
            ],
            out_specs=pl.BlockSpec((count * tokens, tile), lambda j, who: (0, j)),
        ),
        compiler_params=pltpu.CompilerParams(vmem_limit_bytes=36 << 20),
        cost_estimate=pl.CostEstimate(flops=1, bytes_accessed=1, transcendentals=0),
    )(who, weights, weights, *rows)


def stack_kernel(*refs):
    out, start = refs[-1], 0
    for rows in refs[:-1]:
        out[start : start + rows.shape[0]] = rows[...]
        start += rows.shape[0]


def stack_rows(pieces, chains):
    rows, columns = sum(piece.shape[0] for piece in pieces), pieces[0].shape[1]
    span = columns // chains
    return pl.pallas_call(
        stack_kernel,
        out_shape=jax.ShapeDtypeStruct((chains, rows, span), pieces[0].dtype),
        grid=(chains,),
        in_specs=[pl.BlockSpec((piece.shape[0], span), lambda j: (0, j)) for piece in pieces],
        out_specs=pl.BlockSpec((None, rows, span), lambda j: (j, 0, 0)),
        compiler_params=pltpu.CompilerParams(vmem_limit_bytes=36 << 20),
        cost_estimate=pl.CostEstimate(flops=1, bytes_accessed=1, transcendentals=0),
    )(*pieces)


def pick_kernel(order, first, second, out):
    rows, width = first.shape[0], out.shape[2]
    for i in range(out.shape[0]):
        start = pl.multiple_of(order[i] * width, width)
        out[i, :rows] = first[:, pl.ds(start, width)]
        out[i, rows:] = second[:, pl.ds(start, width)]


def pick_columns(values, order, width):
    rows = values[0].shape[0]
    return pl.pallas_call(
        pick_kernel,
        out_shape=jax.ShapeDtypeStruct((order.shape[0], 2 * rows, width), values[0].dtype),
        in_specs=[
            pl.BlockSpec(memory_space=pltpu.SMEM),
            pl.BlockSpec(memory_space=pltpu.VMEM),
            pl.BlockSpec(memory_space=pltpu.VMEM),
        ],
        out_specs=pl.BlockSpec(memory_space=pltpu.VMEM),
    )(order, *values)


def per_device(
    teacher_in,
    routes,
    route_weights,
    expert_gate_up,
    expert_down,
    student_in,
    norm_gain,
    projector,
    second_moment,
):
    bf16, f32 = jnp.bfloat16, jnp.float32
    experts, shares = lax.axis_size("expert"), lax.axis_size("fsdp")
    chips = experts // CORES
    ring, around, back, swap = moves(chips)
    tokens_here, width = teacher_in.shape
    columns = projector.shape[1]
    features = student_in.shape[1]
    hidden_units = expert_down.shape[1]
    lanes = -(-2 * experts // 128) * 128

    me = lax.axis_index("expert")
    share = lax.axis_index("fsdp")

    def fsdp_shift(value, by):
        return lax.ppermute(value, "fsdp", [(i, (i + by) % shares) for i in range(shares)])

    rows = rows_with_weights(teacher_in, routes, route_weights, experts, lanes)
    rows, student_in, expert_gate_up, expert_down, projector = fence(
        (rows, student_in, expert_gate_up, expert_down, projector)
    )
    who = me.reshape(1).astype(jnp.int32)

    student_wide = student_in.astype(f32)
    inv_rms = lax.rsqrt(jnp.mean(student_wide * student_wide, axis=1, keepdims=True) + 1e-06)
    normed = student_wide * inv_rms
    student_feat = (normed * norm_gain[None, :]).astype(bf16)

    block_features = features // experts
    steps = [
        [CORES * ring[(ring.index(q) + (by if core else -by)) % chips] + core for by in range(chips)]
        for q in range(chips)
        for core in range(CORES)
    ]
    steps = lax.dynamic_index_in_dim(jnp.asarray(steps, jnp.int32), me, keepdims=False)

    def feature_blocks(values):
        if block_features % 128:
            value = jnp.concatenate(values, axis=0)
            return value.reshape(value.shape[0], experts, block_features)[:, steps].swapaxes(0, 1)
        return pick_columns(values, steps, block_features)

    down = expert_down[0]
    reach = chips // 2
    cuts = [0, hidden_units * 7 // 16, hidden_units]
    chains = 2
    span = columns // chains
    parts = [slice(chain * span, (chain + 1) * span) for chain in range(chains)]

    def swap_cores(value):
        return lax.ppermute(value, "expert", swap)

    def gather_shares(value):
        return [value] + [fsdp_shift(value, by) for by in range(1, shares)]

    def down_part(down, low, high, by):
        start = lax.rem(share + by, shares) * columns
        return lax.dynamic_slice(down, (low, start), (high - low, columns))

    def hidden_both(rows, swapped):
        return hidden_of(who, weights, [*rows, *swapped], experts)

    def swap_units(gathered):
        units = []
        for value in gathered:
            half = value.shape[0] // 2
            units += [value[:half], swap_cores(value[half:])]
        return jnp.concatenate(units, axis=1)

    def payload(block, sums):
        group = next(group for group in units if block in group)
        start = group.index(block) * tokens_here
        value = units[group][start : start + tokens_here]
        total = [jnp.dot(value, down_rows[chain], preferred_element_type=f32) for chain in range(chains)]
        return [
            mine if value is None else mine + value.astype(f32) for mine, value in zip(total, sums)
        ]

    def send(sums):
        return [lax.ppermute(value.astype(bf16), "expert", around) for value in sums]

    def ring_sums(part_of, held):
        ahead = lax.ppermute(part_of(reach).astype(bf16), "expert", around)
        ahead, held = fence((ahead, held))
        behind = None
        for step in range(reach - 1, 0, -1):
            mine, yours = part_of(chips - step) + ahead.astype(f32), part_of(step)
            if behind is not None:
                yours = yours + behind.astype(f32)
            ahead = lax.ppermute(mine.astype(bf16), "expert", around)
            behind = lax.ppermute(yours.astype(bf16), "expert", back)
        return part_of(0) + ahead.astype(f32) + behind.astype(f32), held

    weights = expert_gate_up.reshape(width, 2 * hidden_units)
    arrived = {0: rows}
    fresh, hidden, gathered, units = [], {}, {}, {}
    far = [[] for _ in range(1, shares)]
    down_rows = near = blocks = projected = swapped = None
    for slot in range(reach):
        incoming = {slot + 1: lax.ppermute(arrived[slot], "expert", around)}
        if slot + 1 < reach:
            incoming[chips - 1 - slot] = lax.ppermute(arrived[-slot % chips], "expert", back)
        next_gathered = {group: gather_shares(value) for group, value in hidden.items() if group != (0,)}
        next_units = {**units, **{group: swap_units(value) for group, value in gathered.items()}}
        next_far = [list(pieces) for pieces in far]
        if slot + 1 < len(cuts):
            for by in range(1, shares):
                part = down_part(down, cuts[slot], cuts[slot + 1], by) if slot == 0 else later_down[by - 1]
                next_far[by - 1].append(fsdp_shift(part, by))
        made = {}
        if slot == 0:
            weights, late_down = fence((weights, down))
            later_down = [down_part(late_down, cuts[1], cuts[2], by) for by in range(1, shares)]
            near = down_part(late_down, 0, hidden_units, 0)
            blocks = feature_blocks((student_feat, swap_cores(student_feat)))
            swapped = swap_cores(rows)
            projected = jnp.dot(student_feat, projector, preferred_element_type=f32)
        else:
            group = tuple(fresh)
            values = [arrived[block] for block in fresh], [swap_cores(arrived[block]) for block in fresh]
            if slot == 1:
                values = [*values[0], *values[1]], [rows, swapped]
            made = {group: hidden_both(*values)}
        if slot == 1:
            near = [near, swap_cores(near)]
        if slot == 2:
            for pieces in far:
                near = [*near, *pieces, *[swap_cores(value) for value in pieces]]
            down_rows = stack_rows(near, chains)
        (later_down, arrived, incoming, swapped, made, gathered, units, far, weights, near, blocks, down_rows, projected) = fence(
            (later_down, arrived, incoming, swapped, made, next_gathered, next_units, next_far, weights, near, blocks, down_rows, projected)
        )
        hidden = made
        if slot == 1:
            (group, value), = made.items()
            start = 2 * len(group) * tokens_here
            hidden = {group: value[:start]}
            own_hidden = value[start:]
        arrived = {**arrived, **incoming}
        fresh = list(incoming)

    def split_group(hidden):
        (group, value), = hidden.items()
        count = len(group)
        value = value.reshape(2, count, tokens_here, hidden_units)
        return {
            (block,): value[:, index].reshape(2 * tokens_here, hidden_units)
            for index, block in enumerate(group)
        }

    sums = [value.astype(bf16) for value in payload(1, [None] * chains)]
    later = split_group(hidden)
    sums, later = fence((sums, later))
    order = [(reach - 1,), (reach,), (reach + 1,)]
    for block in range(1, reach):
        sums = send(sums)
        next_units = {group: swap_units(value) for group, value in gathered.items()}
        gathered = {}
        if order:
            group = order.pop(0)
            gathered[group] = gather_shares(later.pop(group))
        if block == 1:
            later[(reach,)] = hidden_both([arrived[reach]], [swap_cores(arrived[reach])])
        sums[0], gathered, later, next_units = fence((sums[0], gathered, later, next_units))
        units = {**units, **next_units}
        sums = [value.astype(bf16) for value in payload(block + 1, sums)]
    gathered[(0,)] = gather_shares(own_hidden)
    for block in range(reach, chips):
        units = {**units, **{group: swap_units(value) for group, value in gathered.items()}}
        gathered = {}
        sums = payload((block + 1) % chips, send(sums))
    sums = [(projected[:, part] - value).astype(bf16) for part, value in zip(parts, sums)]
    residue = jnp.concatenate(sums, axis=1)

    grads, late_residue = [], residue
    for value in sums:
        both = jnp.concatenate([value, swap_cores(value)], axis=0)

        def grad_part(block):
            return jnp.einsum("tr,tc->rc", blocks[block], both, preferred_element_type=f32)

        grad, late_residue = ring_sums(grad_part, late_residue)
        grads.append(grad)
    grad_block = jnp.concatenate(grads, axis=1)
    feat_part = jnp.einsum("tc,dc->td", late_residue, projector, preferred_element_type=f32).astype(bf16)
    feat_grad = feat_part.astype(f32)
    for by in range(1, shares):
        feat_grad = feat_grad + fsdp_shift(feat_part, by).astype(f32)
    scaled = feat_grad * norm_gain[None, :]
    d_student = (
        inv_rms * (scaled - normed * jnp.mean(scaled * normed, axis=1, keepdims=True))
    ).astype(bf16)

    proj_step = grad_block / jnp.sqrt(
        beta_two * second_moment + (1.0 - beta_two) * grad_block * grad_block
    )
    return (d_student, proj_step)


def solution(mesh):
    placed = (
        P("expert", None),
        P("expert", None),
        P("expert", None),
        P("expert", None, None, "fsdp"),
        P("expert", "fsdp", None),
        P("expert", None),
        P(),
        P(None, "fsdp"),
        P("expert", "fsdp"),
    )
    return jax.shard_map(
        per_device,
        mesh=mesh,
        in_specs=placed,
        out_specs=(P("expert", None), P("expert", "fsdp")),
        check_vma=False,
    )
```

```python
import jax
import jax.numpy as jnp
from jax import lax
from jax.experimental import pallas as pl
from jax.experimental.pallas import tpu as pltpu
from jax.sharding import PartitionSpec as P

beta_two = 0.95
CORES = 2


def ring_order(chips):
    return list(range(0, chips, 2)) + list(range(1, chips, 2))[::-1]


def moves(chips):
    ring = ring_order(chips)
    around = []
    for i in range(chips):
        around.append((CORES * ring[i], CORES * ring[(i + 1) % chips]))
        around.append((CORES * ring[i] + 1, CORES * ring[i - 1] + 1))
    back = [(to, source) for source, to in around]
    return ring, around, back, [(i, i ^ 1) for i in range(CORES * chips)]


def fence(values):
    return lax.optimization_barrier(values)


def rows_kernel(routes, route_weights, tokens, rows, *, experts):
    width, lanes = tokens.shape[1], rows.shape[1] - tokens.shape[1]
    rows[:, :width] = tokens[...]
    column = lax.broadcasted_iota(jnp.int32, (lanes, tokens.shape[0]), 0)
    weight = jnp.zeros(column.shape, jnp.float32)
    for k in range(routes.shape[0]):
        route = routes[k : k + 1, :]
        hit = (column == route) | (column == route + experts)
        weight = weight + jnp.where(hit, route_weights[k : k + 1, :], 0.0)
    high = weight.astype(jnp.bfloat16).astype(jnp.float32)
    weight = jnp.where(column < experts, high, weight - high)
    rows[:, width:] = weight.T.astype(jnp.bfloat16)


def rows_with_weights(tokens, routes, route_weights, experts, lanes):
    return pl.pallas_call(
        lambda *refs: rows_kernel(*refs, experts=experts),
        out_shape=jax.ShapeDtypeStruct((tokens.shape[0], tokens.shape[1] + lanes), tokens.dtype),
    )(routes.T, route_weights.T, tokens)


def hidden_kernel(who, gates, ups, *refs, experts):
    rows, hidden = refs[:-1], refs[-1]
    tokens, width = rows[0].shape[0], gates.shape[0]
    lane = lax.broadcasted_iota(jnp.int32, (tokens, rows[0].shape[1] - width), 1)
    mine = (lane == who[0]) | (lane == who[0] + experts)
    for index, block in enumerate(rows):
        gate = jnp.dot(block[:, :width], gates[...], preferred_element_type=jnp.float32)
        up = jnp.dot(block[:, :width], ups[...], preferred_element_type=jnp.float32)
        weight = jnp.where(mine, block[:, width:].astype(jnp.float32), 0.0)
        weight = jnp.sum(weight, axis=1, keepdims=True)
        out = gate / (1.0 + jnp.exp(-gate)) * up * weight
        hidden[index * tokens : (index + 1) * tokens] = out.astype(hidden.dtype)


def hidden_of(who, weights, rows, experts):
    width, both = weights.shape
    tokens, count = rows[0].shape[0], len(rows)
    tile = min(both // 2, 256)
    tiles = both // 2 // tile
    return pl.pallas_call(
        lambda *refs: hidden_kernel(*refs, experts=experts),
        out_shape=jax.ShapeDtypeStruct((count * tokens, both // 2), jnp.bfloat16),
        grid_spec=pltpu.PrefetchScalarGridSpec(
            num_scalar_prefetch=1,
            grid=(tiles,),
            in_specs=[
                pl.BlockSpec((width, tile), lambda j, who: (0, j)),
                pl.BlockSpec((width, tile), lambda j, who: (0, tiles + j)),
                *[pl.BlockSpec(block.shape, lambda j, who: (0, 0)) for block in rows],
            ],
            out_specs=pl.BlockSpec((count * tokens, tile), lambda j, who: (0, j)),
        ),
        compiler_params=pltpu.CompilerParams(vmem_limit_bytes=28 << 20),
        cost_estimate=pl.CostEstimate(flops=1, bytes_accessed=1, transcendentals=0),
    )(who, weights, weights, *rows)


def stack_kernel(*refs):
    out, start = refs[-1], 0
    for rows in refs[:-1]:
        out[start : start + rows.shape[0]] = rows[...]
        start += rows.shape[0]


def stack_rows(pieces, chains):
    rows, columns = sum(piece.shape[0] for piece in pieces), pieces[0].shape[1]
    span = columns // chains
    return pl.pallas_call(
        stack_kernel,
        out_shape=jax.ShapeDtypeStruct((chains, rows, span), pieces[0].dtype),
        grid=(chains,),
        in_specs=[pl.BlockSpec((piece.shape[0], span), lambda j: (0, j)) for piece in pieces],
        out_specs=pl.BlockSpec((None, rows, span), lambda j: (j, 0, 0)),
        compiler_params=pltpu.CompilerParams(vmem_limit_bytes=28 << 20),
        cost_estimate=pl.CostEstimate(flops=1, bytes_accessed=1, transcendentals=0),
    )(*pieces)


def pick_kernel(order, first, second, out):
    rows, width = first.shape[0], out.shape[2]
    for i in range(out.shape[0]):
        start = pl.multiple_of(order[i] * width, width)
        out[i, :rows] = first[:, pl.ds(start, width)]
        out[i, rows:] = second[:, pl.ds(start, width)]


def pick_columns(values, order, width):
    rows = values[0].shape[0]
    return pl.pallas_call(
        pick_kernel,
        out_shape=jax.ShapeDtypeStruct((order.shape[0], 2 * rows, width), values[0].dtype),
        in_specs=[
            pl.BlockSpec(memory_space=pltpu.SMEM),
            pl.BlockSpec(memory_space=pltpu.VMEM),
            pl.BlockSpec(memory_space=pltpu.VMEM),
        ],
        out_specs=pl.BlockSpec(memory_space=pltpu.VMEM),
    )(order, *values)


def per_device(
    teacher_in,
    routes,
    route_weights,
    expert_gate_up,
    expert_down,
    student_in,
    norm_gain,
    projector,
    second_moment,
):
    bf16, f32 = jnp.bfloat16, jnp.float32
    experts, shares = lax.axis_size("expert"), lax.axis_size("fsdp")
    chips = experts // CORES
    ring, around, back, swap = moves(chips)
    tokens_here, width = teacher_in.shape
    columns = projector.shape[1]
    features = student_in.shape[1]
    hidden_units = expert_down.shape[1]
    lanes = -(-2 * experts // 128) * 128

    me = lax.axis_index("expert")
    share = lax.axis_index("fsdp")

    def fsdp_shift(value, by):
        return lax.ppermute(value, "fsdp", [(i, (i + by) % shares) for i in range(shares)])

    rows = rows_with_weights(teacher_in, routes, route_weights, experts, lanes)
    rows, expert_gate_up, expert_down = fence((rows, expert_gate_up, expert_down))
    weights = expert_gate_up.reshape(width, -1)
    weights, late_down, student_in, projector = fence((weights, expert_down[0], student_in, projector))
    who = me.reshape(1).astype(jnp.int32)

    student_wide = student_in.astype(f32)
    inv_rms = lax.rsqrt(jnp.mean(student_wide * student_wide, axis=1, keepdims=True) + 1e-06)
    normed = student_wide * inv_rms
    student_feat = (normed * norm_gain[None, :]).astype(bf16)

    block_features = features // experts
    steps = [
        [CORES * ring[(ring.index(q) + (by if core else -by)) % chips] + core for by in range(chips)]
        for q in range(chips)
        for core in range(CORES)
    ]
    steps = lax.dynamic_index_in_dim(jnp.asarray(steps, jnp.int32), me, keepdims=False)

    def feature_blocks(values):
        if block_features % 128:
            value = jnp.concatenate(values, axis=0)
            return value.reshape(value.shape[0], experts, block_features)[:, steps].swapaxes(0, 1)
        return pick_columns(values, steps, block_features)

    down = expert_down[0]
    reach = chips // 2
    cuts = [0, hidden_units * 7 // 16, hidden_units]
    chains = 2
    span = columns // chains
    parts = [slice(chain * span, (chain + 1) * span) for chain in range(chains)]

    def swap_cores(value):
        return lax.ppermute(value, "expert", swap)

    def gather_shares(value):
        return [value] + [fsdp_shift(value, by) for by in range(1, shares)]

    def down_part(down, low, high, by):
        start = lax.rem(share + by, shares) * columns
        return lax.dynamic_slice(down, (low, start), (high - low, columns))

    def hidden_both(rows, swapped):
        return hidden_of(who, weights, [*rows, *swapped], experts)

    def swap_units(gathered):
        units = []
        for value in gathered:
            half = value.shape[0] // 2
            units += [value[:half], swap_cores(value[half:])]
        return jnp.concatenate(units, axis=1)

    def payload(block, sums):
        group = next(group for group in units if block in group)
        start = group.index(block) * tokens_here
        value = units[group][start : start + tokens_here]
        total = [jnp.dot(value, down_rows[chain], preferred_element_type=f32) for chain in range(chains)]
        return [
            mine if value is None else mine + value.astype(f32) for mine, value in zip(total, sums)
        ]

    def send(sums):
        return [lax.ppermute(value.astype(bf16), "expert", around) for value in sums]

    def ring_sums(part_of, held):
        ahead = lax.ppermute(part_of(reach).astype(bf16), "expert", around)
        ahead, held = fence((ahead, held))
        behind = None
        for step in range(reach - 1, 0, -1):
            mine, yours = part_of(chips - step) + ahead.astype(f32), part_of(step)
            if behind is not None:
                yours = yours + behind.astype(f32)
            ahead = lax.ppermute(mine.astype(bf16), "expert", around)
            behind = lax.ppermute(yours.astype(bf16), "expert", back)
        return part_of(0) + ahead.astype(f32) + behind.astype(f32), held

    arrived = {0: rows}
    fresh, hidden, gathered, units = [], {}, {}, {}
    far = [[] for _ in range(1, shares)]
    down_rows = near = blocks = projected = swapped = None
    for slot in range(reach):
        incoming = {slot + 1: lax.ppermute(arrived[slot], "expert", around)}
        if slot + 1 < reach:
            incoming[chips - 1 - slot] = lax.ppermute(arrived[-slot % chips], "expert", back)
        next_gathered = {group: gather_shares(value) for group, value in hidden.items() if group != (0,)}
        next_units = {**units, **{group: swap_units(value) for group, value in gathered.items()}}
        next_far = [list(pieces) for pieces in far]
        if slot + 1 < len(cuts):
            for by in range(1, shares):
                part = down_part(down, cuts[slot], cuts[slot + 1], by) if slot == 0 else later_down[by - 1]
                next_far[by - 1].append(fsdp_shift(part, by))
        made = {}
        if slot == 0:
            later_down = [down_part(late_down, cuts[1], cuts[2], by) for by in range(1, shares)]
            near = down_part(late_down, 0, hidden_units, 0)
            blocks = feature_blocks((student_feat, swap_cores(student_feat)))
            swapped = swap_cores(rows)
        else:
            group = tuple(fresh)
            values = [arrived[block] for block in fresh], [swap_cores(arrived[block]) for block in fresh]
            if slot == 1:
                values = [*values[0], *values[1]], [rows, swapped]
            made = {group: hidden_both(*values)}
        if slot == 1:
            near = [near, swap_cores(near)]
            projected = jnp.dot(student_feat, projector, preferred_element_type=f32)
        if slot == 2:
            for pieces in far:
                near = [*near, *pieces, *[swap_cores(value) for value in pieces]]
            down_rows = stack_rows(near, chains)
        (later_down, arrived, incoming, swapped, made, gathered, units, far, weights, near, blocks, down_rows, projected) = fence(
            (later_down, arrived, incoming, swapped, made, next_gathered, next_units, next_far, weights, near, blocks, down_rows, projected)
        )
        hidden = made
        if slot == 1:
            (group, value), = made.items()
            start = 2 * len(group) * tokens_here
            hidden = {group: value[:start]}
            own_hidden = value[start:]
        arrived = {**arrived, **incoming}
        fresh = list(incoming)

    def split_group(hidden):
        (group, value), = hidden.items()
        count = len(group)
        value = value.reshape(2, count, tokens_here, hidden_units)
        return {
            (block,): value[:, index].reshape(2 * tokens_here, hidden_units)
            for index, block in enumerate(group)
        }

    sums = [value.astype(bf16) for value in payload(1, [None] * chains)]
    later = split_group(hidden)
    sums, later = fence((sums, later))
    order = [(reach - 1,), (reach,), (reach + 1,)]
    for block in range(1, reach):
        sums = send(sums)
        next_units = {group: swap_units(value) for group, value in gathered.items()}
        gathered = {}
        if order:
            group = order.pop(0)
            gathered[group] = gather_shares(later.pop(group))
        if block == 1:
            later[(reach,)] = hidden_both([arrived[reach]], [swap_cores(arrived[reach])])
        sums[0], gathered, later, next_units = fence((sums[0], gathered, later, next_units))
        units = {**units, **next_units}
        sums = [value.astype(bf16) for value in payload(block + 1, sums)]
    gathered[(0,)] = gather_shares(own_hidden)
    for block in range(reach, chips):
        units = {**units, **{group: swap_units(value) for group, value in gathered.items()}}
        gathered = {}
        sums = payload((block + 1) % chips, send(sums))
    sums = [(projected[:, part] - value).astype(bf16) for part, value in zip(parts, sums)]
    residue = jnp.concatenate(sums, axis=1)

    grads, late_residue = [], residue
    for value in sums:
        both = jnp.concatenate([value, swap_cores(value)], axis=0)

        def grad_part(block):
            return jnp.einsum("tr,tc->rc", blocks[block], both, preferred_element_type=f32)

        grad, late_residue = ring_sums(grad_part, late_residue)
        grads.append(grad)
    grad_block = jnp.concatenate(grads, axis=1)
    feat_part = jnp.einsum("tc,dc->td", late_residue, projector, preferred_element_type=f32).astype(bf16)
    feat_grad = feat_part.astype(f32)
    for by in range(1, shares):
        feat_grad = feat_grad + fsdp_shift(feat_part, by).astype(f32)
    scaled = feat_grad * norm_gain[None, :]
    d_student = (
        inv_rms * (scaled - normed * jnp.mean(scaled * normed, axis=1, keepdims=True))
    ).astype(bf16)

    proj_step = grad_block / jnp.sqrt(
        beta_two * second_moment + (1.0 - beta_two) * grad_block * grad_block
    )
    return (d_student, proj_step)


def solution(mesh):
    placed = (
        P("expert", None),
        P("expert", None),
        P("expert", None),
        P("expert", None, None, "fsdp"),
        P("expert", "fsdp", None),
        P("expert", None),
        P(),
        P(None, "fsdp"),
        P("expert", "fsdp"),
    )
    return jax.shard_map(
        per_device,
        mesh=mesh,
        in_specs=placed,
        out_specs=(P("expert", None), P("expert", "fsdp")),
        check_vma=False,
    )
```

```python
import jax
import jax.numpy as jnp
from jax import lax
from jax.experimental import pallas as pl
from jax.experimental.pallas import tpu as pltpu
from jax.sharding import PartitionSpec as P

beta_two = 0.95
CORES = 2


def ring_order(chips):
    return list(range(0, chips, 2)) + list(range(1, chips, 2))[::-1]


def moves(chips):
    ring = ring_order(chips)
    around = []
    for i in range(chips):
        around.append((CORES * ring[i], CORES * ring[(i + 1) % chips]))
        around.append((CORES * ring[i] + 1, CORES * ring[i - 1] + 1))
    back = [(to, source) for source, to in around]
    return ring, around, back, [(i, i ^ 1) for i in range(CORES * chips)]


def fence(values):
    return lax.optimization_barrier(values)


def rows_kernel(routes, route_weights, tokens, rows, *, experts):
    width, lanes = tokens.shape[1], rows.shape[1] - tokens.shape[1]
    rows[:, :width] = tokens[...]
    column = lax.broadcasted_iota(jnp.int32, (lanes, tokens.shape[0]), 0)
    weight = jnp.zeros(column.shape, jnp.float32)
    for k in range(routes.shape[0]):
        route = routes[k : k + 1, :]
        hit = (column == route) | (column == route + experts)
        weight = weight + jnp.where(hit, route_weights[k : k + 1, :], 0.0)
    high = weight.astype(jnp.bfloat16).astype(jnp.float32)
    weight = jnp.where(column < experts, high, weight - high)
    rows[:, width:] = weight.T.astype(jnp.bfloat16)


def rows_with_weights(tokens, routes, route_weights, experts, lanes):
    return pl.pallas_call(
        lambda *refs: rows_kernel(*refs, experts=experts),
        out_shape=jax.ShapeDtypeStruct((tokens.shape[0], tokens.shape[1] + lanes), tokens.dtype),
    )(routes.T, route_weights.T, tokens)


def hidden_kernel(who, gates, ups, *refs, experts):
    rows, hidden = refs[:-1], refs[-1]
    tokens, width = rows[0].shape[0], gates.shape[0]
    lane = lax.broadcasted_iota(jnp.int32, (tokens, rows[0].shape[1] - width), 1)
    mine = (lane == who[0]) | (lane == who[0] + experts)
    for index, block in enumerate(rows):
        gate = jnp.dot(block[:, :width], gates[...], preferred_element_type=jnp.float32)
        up = jnp.dot(block[:, :width], ups[...], preferred_element_type=jnp.float32)
        weight = jnp.where(mine, block[:, width:].astype(jnp.float32), 0.0)
        weight = jnp.sum(weight, axis=1, keepdims=True)
        out = gate / (1.0 + jnp.exp(-gate)) * up * weight
        hidden[index * tokens : (index + 1) * tokens] = out.astype(hidden.dtype)


def hidden_of(who, weights, rows, experts):
    width, both = weights.shape
    tokens, count = rows[0].shape[0], len(rows)
    tile = min(both // 2, 256)
    tiles = both // 2 // tile
    return pl.pallas_call(
        lambda *refs: hidden_kernel(*refs, experts=experts),
        out_shape=jax.ShapeDtypeStruct((count * tokens, both // 2), jnp.bfloat16),
        grid_spec=pltpu.PrefetchScalarGridSpec(
            num_scalar_prefetch=1,
            grid=(tiles,),
            in_specs=[
                pl.BlockSpec((width, tile), lambda j, who: (0, j)),
                pl.BlockSpec((width, tile), lambda j, who: (0, tiles + j)),
                *[pl.BlockSpec(block.shape, lambda j, who: (0, 0)) for block in rows],
            ],
            out_specs=pl.BlockSpec((count * tokens, tile), lambda j, who: (0, j)),
        ),
        compiler_params=pltpu.CompilerParams(vmem_limit_bytes=28 << 20),
        cost_estimate=pl.CostEstimate(flops=1, bytes_accessed=1, transcendentals=0),
    )(who, weights, weights, *rows)


def stack_kernel(*refs):
    out, start = refs[-1], 0
    for rows in refs[:-1]:
        out[start : start + rows.shape[0]] = rows[...]
        start += rows.shape[0]


def stack_rows(pieces, chains):
    rows, columns = sum(piece.shape[0] for piece in pieces), pieces[0].shape[1]
    span = columns // chains
    return pl.pallas_call(
        stack_kernel,
        out_shape=jax.ShapeDtypeStruct((chains, rows, span), pieces[0].dtype),
        grid=(chains,),
        in_specs=[pl.BlockSpec((piece.shape[0], span), lambda j: (0, j)) for piece in pieces],
        out_specs=pl.BlockSpec((None, rows, span), lambda j: (j, 0, 0)),
        compiler_params=pltpu.CompilerParams(vmem_limit_bytes=28 << 20),
        cost_estimate=pl.CostEstimate(flops=1, bytes_accessed=1, transcendentals=0),
    )(*pieces)


def pick_kernel(order, first, second, out):
    rows, width = first.shape[0], out.shape[2]
    for i in range(out.shape[0]):
        start = pl.multiple_of(order[i] * width, width)
        out[i, :rows] = first[:, pl.ds(start, width)]
        out[i, rows:] = second[:, pl.ds(start, width)]


def pick_columns(values, order, width):
    rows = values[0].shape[0]
    return pl.pallas_call(
        pick_kernel,
        out_shape=jax.ShapeDtypeStruct((order.shape[0], 2 * rows, width), values[0].dtype),
        in_specs=[
            pl.BlockSpec(memory_space=pltpu.SMEM),
            pl.BlockSpec(memory_space=pltpu.VMEM),
            pl.BlockSpec(memory_space=pltpu.VMEM),
        ],
        out_specs=pl.BlockSpec(memory_space=pltpu.VMEM),
    )(order, *values)


def per_device(
    teacher_in,
    routes,
    route_weights,
    expert_gate_up,
    expert_down,
    student_in,
    norm_gain,
    projector,
    second_moment,
):
    bf16, f32 = jnp.bfloat16, jnp.float32
    experts, shares = lax.axis_size("expert"), lax.axis_size("fsdp")
    chips = experts // CORES
    ring, around, back, swap = moves(chips)
    tokens_here, width = teacher_in.shape
    columns = projector.shape[1]
    features = student_in.shape[1]
    hidden_units = expert_down.shape[1]
    lanes = -(-2 * experts // 128) * 128

    me = lax.axis_index("expert")
    share = lax.axis_index("fsdp")

    def fsdp_shift(value, by):
        return lax.ppermute(value, "fsdp", [(i, (i + by) % shares) for i in range(shares)])

    rows = rows_with_weights(teacher_in, routes, route_weights, experts, lanes)
    rows, expert_gate_up, expert_down = fence((rows, expert_gate_up, expert_down))
    weights = expert_gate_up.reshape(width, -1)
    weights, late_down, student_in, projector = fence((weights, expert_down[0], student_in, projector))
    who = me.reshape(1).astype(jnp.int32)

    student_wide = student_in.astype(f32)
    inv_rms = lax.rsqrt(jnp.mean(student_wide * student_wide, axis=1, keepdims=True) + 1e-06)
    normed = student_wide * inv_rms
    student_feat = (normed * norm_gain[None, :]).astype(bf16)

    block_features = features // experts
    steps = [
        [CORES * ring[(ring.index(q) + (by if core else -by)) % chips] + core for by in range(chips)]
        for q in range(chips)
        for core in range(CORES)
    ]
    steps = lax.dynamic_index_in_dim(jnp.asarray(steps, jnp.int32), me, keepdims=False)

    def feature_blocks(values):
        if block_features % 128:
            value = jnp.concatenate(values, axis=0)
            return value.reshape(value.shape[0], experts, block_features)[:, steps].swapaxes(0, 1)
        return pick_columns(values, steps, block_features)

    down = expert_down[0]
    reach = chips // 2
    cuts = [0, hidden_units * 7 // 16, hidden_units]
    chains = 2
    span = columns // chains
    parts = [slice(chain * span, (chain + 1) * span) for chain in range(chains)]

    def swap_cores(value):
        return lax.ppermute(value, "expert", swap)

    def gather_shares(value):
        half = value.shape[0] // 2
        near = [value[:half], swap_cores(value[half:])]
        return near, [fsdp_shift(value, by) for by in range(1, shares)]

    def down_part(down, low, high, by):
        start = lax.rem(share + by, shares) * columns
        return lax.dynamic_slice(down, (low, start), (high - low, columns))

    def hidden_both(rows, swapped):
        return hidden_of(who, weights, [*rows, *swapped], experts)

    def swap_units(gathered):
        near, others = gathered
        units = [*near]
        for value in others:
            half = value.shape[0] // 2
            units += [value[:half], swap_cores(value[half:])]
        return jnp.concatenate(units, axis=1)

    def payload(block, sums):
        group = next(group for group in units if block in group)
        start = group.index(block) * tokens_here
        value = units[group][start : start + tokens_here]
        total = [jnp.dot(value, down_rows[chain], preferred_element_type=f32) for chain in range(chains)]
        return [
            mine if value is None else mine + value.astype(f32) for mine, value in zip(total, sums)
        ]

    def send(sums):
        return [lax.ppermute(value.astype(bf16), "expert", around) for value in sums]

    def ring_sums(part_of, held):
        ahead = lax.ppermute(part_of(reach).astype(bf16), "expert", around)
        if held is not None:
            ahead, held = fence((ahead, held))
        behind = None
        for step in range(reach - 1, 0, -1):
            mine, yours = part_of(chips - step) + ahead.astype(f32), part_of(step)
            if behind is not None:
                yours = yours + behind.astype(f32)
            ahead = lax.ppermute(mine.astype(bf16), "expert", around)
            behind = lax.ppermute(yours.astype(bf16), "expert", back)
        return part_of(0) + ahead.astype(f32) + behind.astype(f32), held

    arrived = {0: rows}
    fresh, hidden, gathered, units = [], {}, {}, {}
    far = [[] for _ in range(1, shares)]
    down_rows = near = blocks = projected = swapped = None
    for slot in range(reach):
        incoming = {slot + 1: lax.ppermute(arrived[slot], "expert", around)}
        if slot + 1 < reach:
            incoming[chips - 1 - slot] = lax.ppermute(arrived[-slot % chips], "expert", back)
        next_gathered = {group: gather_shares(value) for group, value in hidden.items() if group != (0,)}
        next_units = {**units, **{group: swap_units(value) for group, value in gathered.items()}}
        next_far = [list(pieces) for pieces in far]
        if slot + 1 < len(cuts):
            for by in range(1, shares):
                part = down_part(down, cuts[slot], cuts[slot + 1], by) if slot == 0 else later_down[by - 1]
                next_far[by - 1].append(fsdp_shift(part, by))
        made = {}
        if slot == 0:
            later_down = [down_part(late_down, cuts[1], cuts[2], by) for by in range(1, shares)]
            near = down_part(late_down, 0, hidden_units, 0)
            blocks = feature_blocks((student_feat, swap_cores(student_feat)))
            swapped = swap_cores(rows)
        else:
            group = tuple(fresh)
            values = [arrived[block] for block in fresh], [swap_cores(arrived[block]) for block in fresh]
            if slot == 1:
                values = [*values[0], *values[1]], [rows, swapped]
            made = {group: hidden_both(*values)}
        if slot == 1:
            near = [near, swap_cores(near)]
            projected = jnp.dot(student_feat, projector, preferred_element_type=f32)
        if slot == 2:
            for pieces in far:
                near = [*near, *pieces, *[swap_cores(value) for value in pieces]]
            down_rows = stack_rows(near, chains)
        (later_down, arrived, incoming, swapped, made, gathered, units, far, weights, near, blocks, down_rows, projected) = fence(
            (later_down, arrived, incoming, swapped, made, next_gathered, next_units, next_far, weights, near, blocks, down_rows, projected)
        )
        hidden = made
        if slot == 1:
            (group, value), = made.items()
            start = 2 * len(group) * tokens_here
            hidden = {group: value[:start]}
            own_hidden = value[start:]
        arrived = {**arrived, **incoming}
        fresh = list(incoming)

    def split_group(hidden):
        (group, value), = hidden.items()
        count = len(group)
        value = value.reshape(2, count, tokens_here, hidden_units)
        return {
            (block,): value[:, index].reshape(2 * tokens_here, hidden_units)
            for index, block in enumerate(group)
        }

    sums = [value.astype(bf16) for value in payload(1, [None] * chains)]
    later = split_group(hidden)
    sums, later = fence((sums, later))
    order = [(reach - 1,), (reach,), (reach + 1,)]
    for block in range(1, reach):
        sums = send(sums)
        next_units = {group: swap_units(value) for group, value in gathered.items()}
        gathered = {}
        if order:
            group = order.pop(0)
            gathered[group] = gather_shares(later.pop(group))
        if block == 1:
            later[(reach,)] = hidden_both([arrived[reach]], [swap_cores(arrived[reach])])
        sums[0], gathered, later, next_units = fence((sums[0], gathered, later, next_units))
        units = {**units, **next_units}
        sums = [value.astype(bf16) for value in payload(block + 1, sums)]
    gathered[(0,)] = gather_shares(own_hidden)
    for block in range(reach, chips):
        units = {**units, **{group: swap_units(value) for group, value in gathered.items()}}
        gathered = {}
        sums = payload((block + 1) % chips, send(sums))
    sums = [(projected[:, part] - value).astype(bf16) for part, value in zip(parts, sums)]
    residue = jnp.concatenate(sums, axis=1)

    grads, late_residue = [], residue
    for value in sums:
        both = jnp.concatenate([value, swap_cores(value)], axis=0)

        def grad_part(block):
            return jnp.einsum("tr,tc->rc", blocks[block], both, preferred_element_type=f32)

        grad, held = ring_sums(grad_part, None if grads else late_residue)
        late_residue = late_residue if grads else held
        grads.append(grad)
    grad_block = jnp.concatenate(grads, axis=1)
    feat_part = jnp.einsum("tc,dc->td", late_residue, projector, preferred_element_type=f32).astype(bf16)
    feat_grad = feat_part.astype(f32)
    for by in range(1, shares):
        feat_grad = feat_grad + fsdp_shift(feat_part, by).astype(f32)
    scaled = feat_grad * norm_gain[None, :]
    d_student = (
        inv_rms * (scaled - normed * jnp.mean(scaled * normed, axis=1, keepdims=True))
    ).astype(bf16)

    proj_step = grad_block / jnp.sqrt(
        beta_two * second_moment + (1.0 - beta_two) * grad_block * grad_block
    )
    return (d_student, proj_step)


def solution(mesh):
    placed = (
        P("expert", None),
        P("expert", None),
        P("expert", None),
        P("expert", None, None, "fsdp"),
        P("expert", "fsdp", None),
        P("expert", None),
        P(),
        P(None, "fsdp"),
        P("expert", "fsdp"),
    )
    return jax.shard_map(
        per_device,
        mesh=mesh,
        in_specs=placed,
        out_specs=(P("expert", None), P("expert", "fsdp")),
        check_vma=False,
    )
```

```python
import jax
import jax.numpy as jnp
from jax import lax
from jax.experimental import pallas as pl
from jax.experimental.pallas import tpu as pltpu
from jax.sharding import PartitionSpec as P

beta_two = 0.95
CORES = 2


def ring_order(chips):
    return list(range(0, chips, 2)) + list(range(1, chips, 2))[::-1]


def moves(chips):
    ring = ring_order(chips)
    around = []
    for i in range(chips):
        around.append((CORES * ring[i], CORES * ring[(i + 1) % chips]))
        around.append((CORES * ring[i] + 1, CORES * ring[i - 1] + 1))
    back = [(to, source) for source, to in around]
    return ring, around, back, [(i, i ^ 1) for i in range(CORES * chips)]


def fence(values):
    return lax.optimization_barrier(values)


def rows_kernel(routes, route_weights, tokens, rows, *, experts):
    width, lanes = tokens.shape[1], rows.shape[1] - tokens.shape[1]
    rows[:, :width] = tokens[...]
    column = lax.broadcasted_iota(jnp.int32, (lanes, tokens.shape[0]), 0)
    weight = jnp.zeros(column.shape, jnp.float32)
    for k in range(routes.shape[0]):
        route = routes[k : k + 1, :]
        hit = (column == route) | (column == route + experts)
        weight = weight + jnp.where(hit, route_weights[k : k + 1, :], 0.0)
    high = weight.astype(jnp.bfloat16).astype(jnp.float32)
    weight = jnp.where(column < experts, high, weight - high)
    rows[:, width:] = weight.T.astype(jnp.bfloat16)


def rows_with_weights(tokens, routes, route_weights, experts, lanes):
    return pl.pallas_call(
        lambda *refs: rows_kernel(*refs, experts=experts),
        out_shape=jax.ShapeDtypeStruct((tokens.shape[0], tokens.shape[1] + lanes), tokens.dtype),
    )(routes.T, route_weights.T, tokens)


def hidden_kernel(who, gates, ups, *refs, experts):
    rows, hidden = refs[:-1], refs[-1]
    tokens, width = rows[0].shape[0], gates.shape[0]
    lane = lax.broadcasted_iota(jnp.int32, (tokens, rows[0].shape[1] - width), 1)
    mine = (lane == who[0]) | (lane == who[0] + experts)
    for index, block in enumerate(rows):
        gate = jnp.dot(block[:, :width], gates[...], preferred_element_type=jnp.float32)
        up = jnp.dot(block[:, :width], ups[...], preferred_element_type=jnp.float32)
        weight = jnp.where(mine, block[:, width:].astype(jnp.float32), 0.0)
        weight = jnp.sum(weight, axis=1, keepdims=True)
        out = gate / (1.0 + jnp.exp(-gate)) * up * weight
        hidden[index * tokens : (index + 1) * tokens] = out.astype(hidden.dtype)


def hidden_of(who, weights, rows, experts):
    width, both = weights.shape
    tokens, count = rows[0].shape[0], len(rows)
    tile = min(both // 2, 256)
    tiles = both // 2 // tile
    return pl.pallas_call(
        lambda *refs: hidden_kernel(*refs, experts=experts),
        out_shape=jax.ShapeDtypeStruct((count * tokens, both // 2), jnp.bfloat16),
        grid_spec=pltpu.PrefetchScalarGridSpec(
            num_scalar_prefetch=1,
            grid=(tiles,),
            in_specs=[
                pl.BlockSpec((width, tile), lambda j, who: (0, j)),
                pl.BlockSpec((width, tile), lambda j, who: (0, tiles + j)),
                *[pl.BlockSpec(block.shape, lambda j, who: (0, 0)) for block in rows],
            ],
            out_specs=pl.BlockSpec((count * tokens, tile), lambda j, who: (0, j)),
        ),
        compiler_params=pltpu.CompilerParams(vmem_limit_bytes=28 << 20),
        cost_estimate=pl.CostEstimate(flops=1, bytes_accessed=1, transcendentals=0),
    )(who, weights, weights, *rows)


def stack_kernel(*refs):
    out, start = refs[-1], 0
    for rows in refs[:-1]:
        out[start : start + rows.shape[0]] = rows[...]
        start += rows.shape[0]


def stack_rows(pieces, chains):
    rows, columns = sum(piece.shape[0] for piece in pieces), pieces[0].shape[1]
    span = columns // chains
    return pl.pallas_call(
        stack_kernel,
        out_shape=jax.ShapeDtypeStruct((chains, rows, span), pieces[0].dtype),
        grid=(chains,),
        in_specs=[pl.BlockSpec((piece.shape[0], span), lambda j: (0, j)) for piece in pieces],
        out_specs=pl.BlockSpec((None, rows, span), lambda j: (j, 0, 0)),
        compiler_params=pltpu.CompilerParams(vmem_limit_bytes=28 << 20),
        cost_estimate=pl.CostEstimate(flops=1, bytes_accessed=1, transcendentals=0),
    )(*pieces)


def pick_kernel(order, first, second, out):
    rows, width = first.shape[0], out.shape[2]
    for i in range(out.shape[0]):
        start = pl.multiple_of(order[i] * width, width)
        out[i, :rows] = first[:, pl.ds(start, width)]
        out[i, rows:] = second[:, pl.ds(start, width)]


def pick_columns(values, order, width):
    rows = values[0].shape[0]
    return pl.pallas_call(
        pick_kernel,
        out_shape=jax.ShapeDtypeStruct((order.shape[0], 2 * rows, width), values[0].dtype),
        in_specs=[
            pl.BlockSpec(memory_space=pltpu.SMEM),
            pl.BlockSpec(memory_space=pltpu.VMEM),
            pl.BlockSpec(memory_space=pltpu.VMEM),
        ],
        out_specs=pl.BlockSpec(memory_space=pltpu.VMEM),
    )(order, *values)


def per_device(
    teacher_in,
    routes,
    route_weights,
    expert_gate_up,
    expert_down,
    student_in,
    norm_gain,
    projector,
    second_moment,
):
    bf16, f32 = jnp.bfloat16, jnp.float32
    experts, shares = lax.axis_size("expert"), lax.axis_size("fsdp")
    chips = experts // CORES
    ring, around, back, swap = moves(chips)
    tokens_here, width = teacher_in.shape
    columns = projector.shape[1]
    features = student_in.shape[1]
    hidden_units = expert_down.shape[1]
    lanes = -(-2 * experts // 128) * 128

    me = lax.axis_index("expert")
    share = lax.axis_index("fsdp")

    def fsdp_shift(value, by):
        return lax.ppermute(value, "fsdp", [(i, (i + by) % shares) for i in range(shares)])

    rows = rows_with_weights(teacher_in, routes, route_weights, experts, lanes)
    rows, expert_gate_up, expert_down = fence((rows, expert_gate_up, expert_down))
    weights = expert_gate_up.reshape(width, -1)
    weights, late_down, student_in, projector = fence((weights, expert_down[0], student_in, projector))
    who = me.reshape(1).astype(jnp.int32)

    student_wide = student_in.astype(f32)
    inv_rms = lax.rsqrt(jnp.mean(student_wide * student_wide, axis=1, keepdims=True) + 1e-06)
    normed = student_wide * inv_rms
    student_feat = (normed * norm_gain[None, :]).astype(bf16)

    block_features = features // experts
    steps = [
        [CORES * ring[(ring.index(q) + (by if core else -by)) % chips] + core for by in range(chips)]
        for q in range(chips)
        for core in range(CORES)
    ]
    steps = lax.dynamic_index_in_dim(jnp.asarray(steps, jnp.int32), me, keepdims=False)

    def feature_blocks(values):
        if block_features % 128:
            value = jnp.concatenate(values, axis=0)
            return value.reshape(value.shape[0], experts, block_features)[:, steps].swapaxes(0, 1)
        return pick_columns(values, steps, block_features)

    down = expert_down[0]
    reach = chips // 2
    cuts = [0, hidden_units * 7 // 16, hidden_units]
    chains = 2
    span = columns // chains
    parts = [slice(chain * span, (chain + 1) * span) for chain in range(chains)]

    def swap_cores(value):
        return lax.ppermute(value, "expert", swap)

    def gather_shares(value):
        half = value.shape[0] // 2
        near = [value[:half], swap_cores(value[half:])]
        return near, [fsdp_shift(value, by) for by in range(1, shares)]

    def down_part(down, low, high, by):
        start = lax.rem(share + by, shares) * columns
        return lax.dynamic_slice(down, (low, start), (high - low, columns))

    def hidden_both(rows, swapped):
        return hidden_of(who, weights, [*rows, *swapped], experts)

    def swap_units(gathered):
        near, others = gathered
        units = [*near]
        for value in others:
            half = value.shape[0] // 2
            units += [value[:half], swap_cores(value[half:])]
        return jnp.concatenate(units, axis=1)

    def payload(block, sums):
        group = next(group for group in units if block in group)
        start = group.index(block) * tokens_here
        value = units[group][start : start + tokens_here]
        total = [jnp.dot(value, down_rows[chain], preferred_element_type=f32) for chain in range(chains)]
        return [
            mine if value is None else mine + value.astype(f32) for mine, value in zip(total, sums)
        ]

    def send(sums):
        return [lax.ppermute(value.astype(bf16), "expert", around) for value in sums]

    def ring_sums(part_of, held):
        ahead = lax.ppermute(part_of(reach).astype(bf16), "expert", around)
        if held is not None:
            ahead, held = fence((ahead, held))
        behind = None
        for step in range(reach - 1, 0, -1):
            mine, yours = part_of(chips - step) + ahead.astype(f32), part_of(step)
            if behind is not None:
                yours = yours + behind.astype(f32)
            ahead = lax.ppermute(mine.astype(bf16), "expert", around)
            behind = lax.ppermute(yours.astype(bf16), "expert", back)
        return part_of(0) + ahead.astype(f32) + behind.astype(f32), held

    arrived = {0: rows}
    fresh, hidden, gathered, units = [], {}, {}, {}
    far = [[] for _ in range(1, shares)]
    down_rows = near = blocks = projected = swapped = None
    for slot in range(reach):
        incoming = {slot + 1: lax.ppermute(arrived[slot], "expert", around)}
        if slot + 1 < reach:
            incoming[chips - 1 - slot] = lax.ppermute(arrived[-slot % chips], "expert", back)
        next_gathered = {group: gather_shares(value) for group, value in hidden.items() if group != (0,)}
        next_units = {**units, **{group: swap_units(value) for group, value in gathered.items()}}
        next_far = [list(pieces) for pieces in far]
        if slot + 1 < len(cuts):
            for by in range(1, shares):
                part = down_part(down, cuts[slot], cuts[slot + 1], by) if slot == 0 else later_down[by - 1]
                next_far[by - 1].append(fsdp_shift(part, by))
        made = {}
        if slot == 0:
            later_down = [down_part(late_down, cuts[1], cuts[2], by) for by in range(1, shares)]
            near = down_part(late_down, 0, hidden_units, 0)
            blocks = feature_blocks((student_feat, swap_cores(student_feat)))
            swapped = swap_cores(rows)
        else:
            group = tuple(fresh)
            values = [arrived[block] for block in fresh], [swap_cores(arrived[block]) for block in fresh]
            if slot == 1:
                values = [*values[0], *values[1]], [rows, swapped]
            made = {group: hidden_both(*values)}
        if slot == 1:
            near = [near, swap_cores(near)]
            projected = jnp.dot(student_feat, projector, preferred_element_type=f32)
        if slot == 2:
            for pieces in far:
                near = [*near, *pieces, *[swap_cores(value) for value in pieces]]
            down_rows = stack_rows(near, chains)
        (later_down, arrived, incoming, swapped, made, gathered, units, far, weights, near, blocks, down_rows, projected) = fence(
            (later_down, arrived, incoming, swapped, made, next_gathered, next_units, next_far, weights, near, blocks, down_rows, projected)
        )
        hidden = made
        if slot == 1:
            (group, value), = made.items()
            start = 2 * len(group) * tokens_here
            hidden = {group: value[:start]}
            own_hidden = value[start:]
        arrived = {**arrived, **incoming}
        fresh = list(incoming)

    sums = [value.astype(bf16) for value in payload(1, [None] * chains)]
    later = dict(hidden)
    sums, later = fence((sums, later))
    order = [*later, (reach,)]
    for block in range(1, reach):
        sums = send(sums)
        next_units = {group: swap_units(value) for group, value in gathered.items()}
        gathered = {}
        if order:
            group = order.pop(0)
            gathered[group] = gather_shares(later.pop(group))
        if block == 1:
            later[(reach,)] = hidden_both([arrived[reach]], [swap_cores(arrived[reach])])
        sums[0], gathered, later, next_units = fence((sums[0], gathered, later, next_units))
        units = {**units, **next_units}
        sums = [value.astype(bf16) for value in payload(block + 1, sums)]
    gathered[(0,)] = gather_shares(own_hidden)
    for block in range(reach, chips):
        units = {**units, **{group: swap_units(value) for group, value in gathered.items()}}
        gathered = {}
        sums = payload((block + 1) % chips, send(sums))
    sums = [(projected[:, part] - value).astype(bf16) for part, value in zip(parts, sums)]
    residue = jnp.concatenate(sums, axis=1)

    grads, late_residue = [], residue
    for value in sums:
        both = jnp.concatenate([value, swap_cores(value)], axis=0)

        def grad_part(block):
            return jnp.einsum("tr,tc->rc", blocks[block], both, preferred_element_type=f32)

        grad, held = ring_sums(grad_part, None if grads else late_residue)
        late_residue = late_residue if grads else held
        grads.append(grad)
    grad_block = jnp.concatenate(grads, axis=1)
    feat_part = jnp.einsum("tc,dc->td", late_residue, projector, preferred_element_type=f32).astype(bf16)
    feat_grad = feat_part.astype(f32)
    for by in range(1, shares):
        feat_grad = feat_grad + fsdp_shift(feat_part, by).astype(f32)
    scaled = feat_grad * norm_gain[None, :]
    d_student = (
        inv_rms * (scaled - normed * jnp.mean(scaled * normed, axis=1, keepdims=True))
    ).astype(bf16)

    proj_step = grad_block / jnp.sqrt(
        beta_two * second_moment + (1.0 - beta_two) * grad_block * grad_block
    )
    return (d_student, proj_step)


def solution(mesh):
    placed = (
        P("expert", None),
        P("expert", None),
        P("expert", None),
        P("expert", None, None, "fsdp"),
        P("expert", "fsdp", None),
        P("expert", None),
        P(),
        P(None, "fsdp"),
        P("expert", "fsdp"),
    )
    return jax.shard_map(
        per_device,
        mesh=mesh,
        in_specs=placed,
        out_specs=(P("expert", None), P("expert", "fsdp")),
        check_vma=False,
    )
```
